1024 devices in a mesh: dp: 64 (over z, x), expert: 16 (over y, core).
Axes of the slice: x: 8, y: 8, z: 8, core: 2. Of those that a mesh axis runs over, the one named last changes fastest.
Arguments:
- tokens: bfloat16 [131072, 2048], P(('dp', 'expert')), may hold values from -6 to 6
- expert_index: int32 [131072, 2], P(('dp', 'expert')), may hold values from 0 to 15, all different within a row; in each aligned block of 128 rows (0 to 127, 128 to 255, ...) at most 20 rows name the same one
- gate_weights: bfloat16 [131072, 2], P(('dp', 'expert')), may hold values from 0.049804688 to 1
- cotangent: bfloat16 [131072, 2048], P(('dp', 'expert')), may hold values from -24 to 24
- w_gate: bfloat16 [16, 2048, 384], P('expert'), may hold values from -0.125 to 0.125
- w_up: bfloat16 [16, 2048, 384], P('expert'), may hold values from -0.125 to 0.125
- w_down: bfloat16 [16, 384, 2048], P('expert'), may hold values from -0.3125 to 0.3125
Outputs:
- token_grad: bfloat16 [131072, 2048], P(('dp', 'expert'))
- down_grad: float32 [16, 384, 2048], P('expert', None, 'dp')
The draws below stay inside these ranges and needn't reach their ends.
Inputs may be any that keep to these rules, and one draw needn't show every extreme that they name: `expert_index`: the 2 experts of a token differ. Within each device's aligned block of 128 tokens no expert is named more than 20 times, and in every draw some block names some expert exactly 20 times.
All inputs are finite; a program needn't handle non-finite values.
Results may differ from the reference program's by a relative error of at most 0.0065.
Values may be sent and summed in bfloat16 or wider, within the bound.
A program may use at most 32 MiB of HBM per device.

```python
import math
import jax
import jax.numpy as jnp
import numpy as np
from jax import lax

D = 2048
FF = 384
TOP = 2
TOK_DEV = 128
EXPERTS = 16
CAP = 20
TOKENS = 131072


def spiked(drawn, rng, source, target, shards_of, factor):
    def block_of(dim):
        return (jnp.arange(drawn.shape[dim]) // (drawn.shape[dim] // shards_of)).reshape((-1,) + (1,) * (drawn.ndim - 1 - dim))

    near = jax.random.permutation(rng, shards_of)[block_of(target)]
    second = (block_of(target) + shards_of // 2) % shards_of
    return jnp.where((block_of(source) == near) | (block_of(source) == second), factor * drawn, drawn)


def level_of(key, extent, split, low, high):
    loudness, own = 1.0, jax.random.fold_in(key, 6)
    for axis_at, blocks in split:
        heights = jnp.exp(jax.random.uniform(jax.random.fold_in(own, axis_at), (blocks,), jnp.float32, low / len(split), high / len(split)))
        loudness = loudness * jnp.repeat(heights, extent[axis_at] // blocks).reshape([-1 if axis == axis_at else 1 for axis in range(len(extent))])
    return loudness


def deal_out(key, own, number, rows, number_of, top, most, lean):
    order = jax.random.permutation(key, number_of)
    heavy_load, usual = load_shares(number_of, rows * top, most, lean, True), load_shares(number_of, rows * top, most, lean, False)
    places = jnp.arange(number_of)

    def named(sizes, offset_by):
        used = int((sizes > 0).sum())
        fixed = max(1, used // 4)
        passed = fixed + (places - fixed + offset_by * (used - fixed)) % max(1, number_of - fixed)
        return jnp.zeros((number_of,), jnp.int32).at[order[jnp.where(places < fixed, places, passed)]].set(jnp.asarray(sizes, jnp.int32))

    sizes = jnp.where(number % 4 == 0, named(heavy_load, number // 4), named(usual, number - number // 4 - 1))
    mixed = jax.random.permutation(jax.random.fold_in(own, 3), number_of)
    source_of, sink = mixed[0:number_of // 2 * 2:2], mixed[1:number_of // 2 * 2:2]
    slack = jnp.minimum(sizes[source_of] - 1, most - sizes[sink]) // 2
    slack = jnp.where((source_of == order[0]) | (sink == order[0]) | (sizes[sink] == 0), 0, jnp.maximum(slack, 0))
    passed = jax.random.randint(jax.random.fold_in(own, 4), (number_of // 2,), 0, 1 << 20) % (slack + 1)
    sizes = sizes.at[source_of].add(-passed).at[sink].add(passed)
    items = jnp.searchsorted(jnp.cumsum(sizes), jnp.arange(rows * top), side="right").astype(jnp.int32)
    grid = items.reshape(top, rows).T
    grid = grid[jax.random.permutation(jax.random.fold_in(own, 1), rows)]
    offset_by = jax.random.randint(jax.random.fold_in(own, 2), (rows, 1), 0, top)
    return jnp.take_along_axis(grid, (jnp.arange(top)[None, :] + offset_by) % top, axis=1)


def load_shares(count, total, reach, lean, full):
    weights = [(1 << 20) // math.isqrt(rank ** lean) + 1 for rank in range(1, count + 1)]
    largest = reach if full else min(reach, max(-(-total // count), total * weights[0] // sum(weights)))
    least = 1 if total - largest >= count - 1 else 0
    holding, surplus = [largest] + [least] * (count - 1), total - largest - least * (count - 1)
    while surplus > 0:
        movable = [i for i in range(1, count) if holding[i] < largest] or [i for i in range(1, count) if holding[i] < reach]
        whole, remaining = sum([weights[i] for i in movable]), surplus
        for i in movable:
            extra = min(reach - holding[i], max(1, remaining * weights[i] // whole), surplus)
            holding[i] = holding[i] + extra
            surplus = surplus - extra
    return np.array(holding)


def scatter_about(key, extent, deviation, most, cuts=(), held_as=jnp.bfloat16):
    result = jax.random.normal(key, extent, jnp.float32) * deviation
    if len(cuts) > 0:
        result = level_of(key, extent, cuts, -0.22, 0.18) * result
    return jnp.clip(result, min=-most, max=most).astype(held_as)


def heavy_noise(stream_key, shape, deviation, limit, pieces, heavy, kind=jnp.bfloat16):
    array = deviation * jax.random.normal(stream_key, shape, jnp.float32)
    if pieces:
        array = array * level_of(stream_key, shape, pieces, -0.22, 0.18)
    return jnp.clip(spiked(array, jax.random.fold_in(stream_key, 3), *heavy), -limit, limit).astype(kind)


def setup_inputs(seed: int = 0) -> dict:
    streams_of = jax.random.split(jax.random.key(seed), 8)
    tokens = scatter_about(streams_of[0], (TOKENS, D), 1.0, 6.0, ((0, 1024),))
    expert_index_keys = jax.random.split(jax.random.fold_in(streams_of[1], 1), TOKENS // TOK_DEV)
    expert_index_turns = jax.random.permutation(jax.random.fold_in(streams_of[1], 3), TOKENS // TOK_DEV)
    expert_index = jax.vmap(lambda own, number: deal_out(jax.random.fold_in(streams_of[1], 2), own, number, TOK_DEV, EXPERTS, TOP, CAP, 2))(expert_index_keys, expert_index_turns).reshape((TOKENS, TOP))
    gate_weights = jnp.clip(0.049804688 + 0.9501953 * jax.random.uniform(streams_of[2], (TOKENS, TOP), jnp.float32) ** level_of(streams_of[2], (TOKENS, TOP), ((0, 1024),), -0.2, 0.2), 0.049804688, 1.0).astype(jnp.bfloat16)
    cotangent = heavy_noise(streams_of[3], (TOKENS, D), 1.0, 24.0, ((0, 1024),), (0, 1, 1024, 6.0))
    w_gate = scatter_about(streams_of[4], (EXPERTS, D, FF), D ** -0.5, 0.125, ((0, 16),))
    w_up = scatter_about(streams_of[5], (EXPERTS, D, FF), D ** -0.5, 0.125, ((0, 16),))
    w_down = scatter_about(streams_of[6], (EXPERTS, FF, D), FF ** -0.5, 0.3125, ((0, 16),))
    return {"tokens": tokens, "expert_index": expert_index, "gate_weights": gate_weights, "cotangent": cotangent, "w_gate": w_gate, "w_up": w_up, "w_down": w_down}


def reference(tokens, expert_index, gate_weights, cotangent, w_gate, w_up, w_down):
    block_count = TOKENS // TOK_DEV
    pair_count = TOK_DEV * TOP
    total_pairs = TOKENS * TOP
    chosen = expert_index.reshape(block_count, pair_count)
    matches = (chosen[:, :, None] == jnp.arange(EXPERTS, dtype=jnp.int32)[None, None, :]).astype(jnp.int32)
    position = jnp.sum((jnp.cumsum(matches, axis=1) - matches) * matches, axis=2).astype(jnp.int32)
    pair_ids = (jnp.arange(block_count, dtype=jnp.int32)[:, None] * pair_count
                + jnp.arange(pair_count, dtype=jnp.int32)[None, :]).astype(jnp.int32)
    block_ids = jnp.broadcast_to(jnp.arange(block_count, dtype=jnp.int32)[:, None], (block_count, pair_count))
    gate_flat = gate_weights.reshape(total_pairs).astype(jnp.float32)

    def expert_step(carry_grads, expert_id):
        is_mine = chosen == expert_id
        slot_target = jnp.where(is_mine, position, CAP).astype(jnp.int32)
        source_ids = jnp.full((block_count, CAP + 1), total_pairs, jnp.int32)
        source_ids = source_ids.at[block_ids, slot_target].set(jnp.where(is_mine, pair_ids, total_pairs).astype(jnp.int32))
        source_ids = source_ids[:, :CAP].reshape(block_count * CAP)
        is_live = source_ids < total_pairs
        safe_ids = jnp.where(is_live, source_ids, 0).astype(jnp.int32)
        token_ids = (safe_ids // TOP).astype(jnp.int32)
        expert_rows = jnp.where(is_live[:, None], tokens[token_ids], jnp.zeros((), tokens.dtype))
        gate_pre = jnp.dot(expert_rows, w_gate[expert_id], preferred_element_type=jnp.float32)
        up_pre = jnp.dot(expert_rows, w_up[expert_id], preferred_element_type=jnp.float32)
        sigmoid_gate = jax.nn.sigmoid(gate_pre)
        silu_gate = gate_pre * sigmoid_gate
        hidden = (silu_gate * up_pre).astype(jnp.bfloat16)
        scaled = (gate_flat[safe_ids][:, None] * cotangent[token_ids].astype(jnp.float32)).astype(jnp.bfloat16)
        scaled = jnp.where(is_live[:, None], scaled, jnp.zeros((), jnp.bfloat16))
        hidden_grad = jnp.dot(scaled, w_down[expert_id].T, preferred_element_type=jnp.float32)
        gate_grad = (hidden_grad * up_pre * sigmoid_gate * (1.0 + gate_pre * (1.0 - sigmoid_gate))).astype(jnp.bfloat16)
        up_grad = (hidden_grad * silu_gate).astype(jnp.bfloat16)
        pair_grad = (jnp.dot(gate_grad, w_gate[expert_id].T, preferred_element_type=jnp.float32)
                     + jnp.dot(up_grad, w_up[expert_id].T, preferred_element_type=jnp.float32)).astype(jnp.bfloat16)
        down_term = jnp.dot(hidden.T, scaled, preferred_element_type=jnp.float32)
        write_ids = jnp.where(is_live, source_ids, total_pairs).astype(jnp.int32)
        carry_grads = carry_grads.at[write_ids].set(pair_grad, mode="drop")
        return carry_grads, down_term

    start_grads = jnp.zeros((total_pairs, D), jnp.bfloat16)
    pair_grads, down_grad = lax.scan(expert_step, start_grads, jnp.arange(EXPERTS, dtype=jnp.int32))

    def block_sum(block_grads):
        return jnp.sum(block_grads.astype(jnp.float32), axis=1).astype(jnp.bfloat16)

    token_grad = lax.map(block_sum, pair_grads.reshape(block_count, TOK_DEV, TOP, D)).reshape(TOKENS, D)
    return token_grad, down_grad
```

```python
import functools

import jax
import jax.numpy as jnp
from jax import lax
from jax.experimental import pallas as pl
from jax.experimental.pallas import tpu as pltpu
from jax.sharding import PartitionSpec as P

MESH = pl.DeviceIdType.MESH
F32 = jnp.float32
BF16 = jnp.bfloat16

SIDE = 8
PEERS = 16
SLOTS = 20
MAIN = 16
SPARE = SLOTS - MAIN
FOLD = MAIN // SPARE
GROUP = 4
CHUNKS = PEERS // GROUP
GM = GROUP * MAIN
GS = GROUP * SPARE
GROWS = GM + GS

NT = (((1,), (1,)), ((), ()))
TN = (((0,), (0,)), ((), ()))


def offsets_of(slot):
    pair = slot // 2
    far = 4 - (pair + 1) // 2
    return far * (2 * (pair & 1) - 1), (slot + 1) & 1


def dot(a, b, dims=(((1,), (0,)), ((), ()))):
    return lax.dot_general(a, b, dims, preferred_element_type=F32)


def body(
    ei_ref, gw_ref, tok_hbm, cot_hbm, wg_hbm, wu_hbm, wd_hbm,
    tg_ref, dg_ref,
    tok, cot, wgu, wd, x_out, x_in, c_out, c_in, r_out, r_in,
    t_main, t_spare, xs, pre, scaled, hidden,
    dt_a, dt_b, r_a, r_b, s_a, s_b, q_a, q_b,
    load_sem, xs_sem, xr_sem, cs_sem, cr_sem, rs_sem, rr_sem,
    a1s, a1r, b1s, b1r, a2s, a2r, b2s, b2r,
):
    width = tok.shape[1]
    rows = tok.shape[0]
    ff = wd.shape[0]
    fold = width // FOLD
    part = width // SIDE
    dp = lax.axis_index("dp")
    ex = lax.axis_index("expert")
    z, x = dp // SIDE, dp % SIDE
    y, core = ex // 2, ex % 2

    loads = [
        pltpu.make_async_copy(tok_hbm, tok, load_sem.at[0]),
        pltpu.make_async_copy(cot_hbm, cot, load_sem.at[1]),
        pltpu.make_async_copy(wg_hbm, wgu.at[:, pl.ds(0, ff)], load_sem.at[2]),
        pltpu.make_async_copy(wu_hbm, wgu.at[:, pl.ds(ff, ff)], load_sem.at[3]),
        pltpu.make_async_copy(wd_hbm, wd, load_sem.at[4]),
    ]
    for load in loads:
        load.start()

    def target(slot, way):
        along, other = offsets_of(slot)
        return (dp, ((y + way * along) & (SIDE - 1)) * 2 + ((core + other) & 1))

    def x_peer(k):
        return (z * SIDE + ((x + k) & (SIDE - 1)), ex)

    def z_peer(k):
        return (((z + k) & (SIDE - 1)) * SIDE + x, ex)

    barrier = pltpu.get_barrier_semaphore()
    for slot in range(PEERS - 1):
        pl.semaphore_signal(barrier, inc=1, device_id=target(slot, 1), device_id_type=MESH)
    for k in range(1, SIDE):
        pl.semaphore_signal(barrier, inc=1, device_id=x_peer(k), device_id_type=MESH)
        pl.semaphore_signal(barrier, inc=1, device_id=z_peer(k), device_id_type=MESH)

    lane_e = lax.broadcasted_iota(jnp.int32, (rows, PEERS), 1)
    first = (ei_ref[:, 0:1] == lane_e).astype(F32)
    second = (ei_ref[:, 1:2] == lane_e).astype(F32)
    chosen = (first + second).astype(BF16)
    gates = gw_ref[...].astype(F32)
    gates = (first * gates[:, 0:1] + second * gates[:, 1:2]).astype(BF16)
    before = lax.broadcasted_iota(jnp.int32, (rows, rows), 1) < lax.broadcasted_iota(
        jnp.int32, (rows, rows), 0
    )
    place = dot(before.astype(F32).astype(BF16), chosen).astype(BF16)

    def expert_at(block):
        along, other = offsets_of(block)
        return ((y + along) & (SIDE - 1)) * 2 + ((core + other) & 1)

    nrow = PEERS * MAIN
    down_i = lax.broadcasted_iota(jnp.int32, (nrow, PEERS), 0)
    pick = (
        expert_at(down_i // MAIN) == lax.broadcasted_iota(jnp.int32, (nrow, PEERS), 1)
    ).astype(F32).astype(BF16)
    named = dot(pick, chosen, NT) > 0.5
    at = dot(pick, place, NT).astype(jnp.int32)
    gate_of = dot(pick, gates, NT)
    row_i = lax.broadcasted_iota(jnp.int32, (nrow, rows), 0)
    hit_main = jnp.where(named & (at == (row_i & (MAIN - 1))), 1.0, 0.0)
    hit_spare = jnp.where(named & (at == MAIN + (row_i & (SPARE - 1))), 1.0, 0.0)
    scale_main = jnp.sum(hit_main * gate_of, axis=1, keepdims=True)
    scale_spare = jnp.sum(hit_spare * gate_of, axis=1, keepdims=True)
    piece_i = (row_i & (MAIN - 1)) // SPARE
    take_main = hit_main.astype(BF16)
    take_spare = [
        jnp.where(piece_i == g, hit_spare, 0.0).astype(BF16) for g in range(FOLD)
    ]
    named_t = dot(chosen, pick, NT) > 0.5
    at_t = dot(place, pick, NT).astype(jnp.int32)
    col_i = lax.broadcasted_iota(jnp.int32, (rows, nrow), 1)
    t_main[...] = jnp.where(named_t & (at_t == (col_i & (MAIN - 1))), 1.0, 0.0).astype(BF16)
    t_spare[...] = jnp.where(
        named_t & (at_t == MAIN + (col_i & (SPARE - 1))), 1.0, 0.0
    ).astype(BF16)

    def gather(source, out, scales):
        for g in range(FOLD):
            cols = slice(g * fold, (g + 1) * fold)
            got = dot(take_main, source[:, cols])
            if scales is not None:
                got = got * scales[0]
            out[:, :, cols] = got.astype(BF16).reshape(PEERS, MAIN, fold)
        got = dot(take_spare[0], source[:, 0:fold])
        for g in range(1, FOLD):
            got = got + dot(take_spare[g], source[:, g * fold : (g + 1) * fold])
        if scales is not None:
            got = got * scales[1]
        out[:, :, width:] = got.astype(BF16).reshape(PEERS, MAIN, fold)

    def move(slot, way, out, into, send, recv):
        return pltpu.make_async_remote_copy(
            src_ref=out.at[slot],
            dst_ref=into.at[slot],
            send_sem=send.at[slot],
            recv_sem=recv.at[slot],
            device_id=target(slot, way),
            device_id_type=MESH,
        )

    own = PEERS - 1
    loads[0].wait()
    gather(tok, x_out, None)
    pl.semaphore_wait(barrier, PEERS - 1 + 2 * (SIDE - 1))
    for slot in range(PEERS - 1):
        move(slot, 1, x_out, x_in, xs_sem, xr_sem).start()
    loads[1].wait()
    gather(cot, c_out, (scale_main, scale_spare))
    for slot in range(PEERS - 1):
        move(slot, 1, c_out, c_in, cs_sem, cr_sem).start()
    x_in[own] = x_out[own]
    c_in[own] = c_out[own]

    big_i = lax.broadcasted_iota(jnp.int32, (GS, GM), 1)
    small_i = lax.broadcasted_iota(jnp.int32, (GS, GM), 0)
    big_t = lax.broadcasted_iota(jnp.int32, (GM, GS), 0)
    small_t = lax.broadcasted_iota(jnp.int32, (GM, GS), 1)

    def unfold(g):
        want = (small_i // SPARE) * MAIN + g * SPARE + (small_i & (SPARE - 1))
        return jnp.where(big_i == want, 1.0, 0.0).astype(BF16)

    def refold(g):
        want = (small_t // SPARE) * MAIN + g * SPARE + (small_t & (SPARE - 1))
        return jnp.where(big_t == want, 1.0, 0.0).astype(BF16)

    def wait_block(slot, way, out, into, send, recv):
        @pl.when(slot < own)
        def _():
            move(slot, way, out, into, send, recv).wait_recv()

    def unpack(into, chunk, dest, base):
        blocks = into.at[pl.ds(chunk * GROUP, GROUP)]
        dest[pl.ds(base, GM), :] = blocks[:, :, 0:width].reshape(GM, width)
        spare = blocks[:, :, width:].reshape(GM, fold)
        for g in range(FOLD):
            dest[pl.ds(base + GM, GS), pl.ds(g * fold, fold)] = dot(unfold(g), spare).astype(BF16)

    loads[2].wait()
    loads[3].wait()

    def forward(chunk, carry):
        for b in range(GROUP):
            wait_block(chunk * GROUP + b, 1, x_out, x_in, xs_sem, xr_sem)
        base = pl.multiple_of(chunk * GROWS, GROWS)
        unpack(x_in, chunk, xs, 0)
        both = dot(xs[...], wgu[...])
        pre[pl.ds(base, GROWS), :] = both
        gate = both[:, 0:ff]
        hidden[pl.ds(base, GROWS), :] = (gate * jax.nn.sigmoid(gate) * both[:, ff:]).astype(BF16)
        return carry

    lax.fori_loop(0, CHUNKS, forward, 0)
    loads[4].wait()

    def backward(chunk, carry):
        for b in range(GROUP):
            wait_block(chunk * GROUP + b, 1, c_out, c_in, cs_sem, cr_sem)
        base = pl.multiple_of(chunk * GROWS, GROWS)
        unpack(c_in, chunk, scaled, base)
        back = dot(scaled[pl.ds(base, GROWS), :], wd[...], NT)
        gate = pre[pl.ds(base, GROWS), 0:ff]
        up = pre[pl.ds(base, GROWS), ff:]
        sig = jax.nn.sigmoid(gate)
        gate_grad = (back * up * sig * (1.0 + gate * (1.0 - sig))).astype(BF16)
        up_grad = (back * (gate * sig)).astype(BF16)
        grads = jnp.concatenate([gate_grad, up_grad], axis=1)
        folded = jnp.zeros((GM, fold), F32)
        for g in range(FOLD):
            cols = pl.ds(g * fold, fold)
            pair = dot(grads, wgu[cols, :], NT).astype(BF16)
            r_out[pl.ds(chunk * GROUP, GROUP), :, cols] = pair[0:GM].reshape(GROUP, MAIN, fold)
            folded = folded + dot(refold(g), pair[GM:])
        r_out[pl.ds(chunk * GROUP, GROUP), :, pl.ds(width, fold)] = folded.astype(BF16).reshape(
            GROUP, MAIN, fold
        )
        for b in range(GROUP):
            slot = chunk * GROUP + b

            @pl.when(slot < own)
            def _():
                move(slot, -1, r_out, r_in, rs_sem, rr_sem).start()

        return carry

    lax.fori_loop(0, CHUNKS, backward, 0)
    r_in[own] = r_out[own]

    half = part // (2 * SIDE)

    def outer(zz, carry):
        cols = pl.ds(pl.multiple_of(zz * part, part), part)
        term = dot(scaled[:, cols], hidden[...], TN).astype(BF16).reshape(SIDE, 2, half, ff)
        for xx in range(SIDE):
            dt_a[xx, zz] = term[xx, 0]
        dt_b[zz] = term[:, 1]
        return carry

    lax.fori_loop(0, SIDE, outer, 0)

    def share(k, peer, at_axis, out, into, send, recv):
        return pltpu.make_async_remote_copy(
            src_ref=out.at[(at_axis + k) & (SIDE - 1)],
            dst_ref=into.at[k - 1],
            send_sem=send.at[k - 1],
            recv_sem=recv.at[k - 1],
            device_id=peer(k),
            device_id_type=MESH,
        )

    order = (4, 3, 5, 2, 6, 1, 7)
    for k in order:
        share(k, x_peer, x, dt_a, r_a, a1s, a1r).start()
        share(k, z_peer, z, dt_b, r_b, b1s, b1r).start()
    for k in order:
        share(k, x_peer, x, dt_a, r_a, a1s, a1r).wait_recv()
    total = dt_a[x].astype(F32)
    for k in range(SIDE - 1):
        total = total + r_a[k].astype(F32)
    s_a[...] = total.astype(BF16)
    for k in order:
        share(k, z_peer, z, s_a, q_a, a2s, a2r).start()
    for k in order:
        share(k, z_peer, z, dt_b, r_b, b1s, b1r).wait_recv()
    total = dt_b[z].astype(F32)
    for k in range(SIDE - 1):
        total = total + r_b[k].astype(F32)
    s_b[...] = total.astype(BF16)
    for k in order:
        share(k, x_peer, x, s_b, q_b, b2s, b2r).start()
    for k in order:
        share(k, z_peer, z, s_a, q_a, a2s, a2r).wait_recv()
        share(k, x_peer, x, s_b, q_b, b2s, b2r).wait_recv()
    total = s_a[z].astype(F32)
    for k in range(SIDE - 1):
        total = total + q_a[k].astype(F32)
    dg_ref[0:half, :] = total
    total = s_b[x].astype(F32)
    for k in range(SIDE - 1):
        total = total + q_b[k].astype(F32)
    dg_ref[half:, :] = total

    for slot in range(PEERS - 1):
        move(slot, -1, r_out, r_in, rs_sem, rr_sem).wait_recv()
    col_piece = (lax.broadcasted_iota(jnp.int32, (rows, nrow), 1) & (MAIN - 1)) // SPARE
    spare = r_in[:, :, width:].reshape(nrow, fold)
    for g in range(FOLD):
        cols = slice(g * fold, (g + 1) * fold)
        main = r_in[:, :, cols].reshape(nrow, fold)
        pick_g = jnp.where(col_piece == g, t_spare[...].astype(F32), 0.0).astype(BF16)
        tg_ref[:, cols] = (dot(t_main[...], main) + dot(pick_g, spare)).astype(BF16)

    for slot in range(PEERS - 1):
        move(slot, 1, x_out, x_in, xs_sem, xr_sem).wait_send()
        move(slot, 1, c_out, c_in, cs_sem, cr_sem).wait_send()
        move(slot, -1, r_out, r_in, rs_sem, rr_sem).wait_send()
    for k in order:
        share(k, x_peer, x, dt_a, r_a, a1s, a1r).wait_send()
        share(k, z_peer, z, dt_b, r_b, b1s, b1r).wait_send()
        share(k, z_peer, z, s_a, q_a, a2s, a2r).wait_send()
        share(k, x_peer, x, s_b, q_b, b2s, b2r).wait_send()


def per_device(tokens, expert_index, gate_weights, cotangent, w_gate, w_up, w_down):
    rows, width = tokens.shape
    ff = w_gate.shape[2]
    wide = width + width // FOLD
    half = width // (2 * SIDE * SIDE)
    vmem = pl.BlockSpec(memory_space=pltpu.VMEM)
    hbm = pl.BlockSpec(memory_space=pl.ANY)
    blocks = pltpu.VMEM((PEERS, MAIN, wide), BF16)
    dma = pltpu.SemaphoreType.DMA
    token_grad, down_t = pl.pallas_call(
        body,
        out_shape=(
            jax.ShapeDtypeStruct((rows, width), BF16),
            jax.ShapeDtypeStruct((2 * half, ff), F32),
        ),
        in_specs=[vmem, vmem, hbm, hbm, hbm, hbm, hbm],
        out_specs=(vmem, vmem),
        scratch_shapes=[
            pltpu.VMEM((rows, width), BF16),
            pltpu.VMEM((rows, width), BF16),
            pltpu.VMEM((width, 2 * ff), BF16),
            pltpu.VMEM((ff, width), BF16),
            blocks, blocks, blocks, blocks, blocks, blocks,
            pltpu.VMEM((rows, PEERS * MAIN), BF16),
            pltpu.VMEM((rows, PEERS * MAIN), BF16),
            pltpu.VMEM((GROWS, width), BF16),
            pltpu.VMEM((CHUNKS * GROWS, 2 * ff), F32),
            pltpu.VMEM((CHUNKS * GROWS, width), BF16),
            pltpu.VMEM((CHUNKS * GROWS, ff), BF16),
            pltpu.VMEM((SIDE, SIDE, half, ff), BF16),
            pltpu.VMEM((SIDE, SIDE, half, ff), BF16),
            pltpu.VMEM((SIDE - 1, SIDE, half, ff), BF16),
            pltpu.VMEM((SIDE - 1, SIDE, half, ff), BF16),
            pltpu.VMEM((SIDE, half, ff), BF16),
            pltpu.VMEM((SIDE, half, ff), BF16),
            pltpu.VMEM((SIDE - 1, half, ff), BF16),
            pltpu.VMEM((SIDE - 1, half, ff), BF16),
            dma((5,)),
            dma((PEERS,)), dma((PEERS,)), dma((PEERS,)), dma((PEERS,)), dma((PEERS,)), dma((PEERS,)),
            dma((SIDE - 1,)), dma((SIDE - 1,)), dma((SIDE - 1,)), dma((SIDE - 1,)),
            dma((SIDE - 1,)), dma((SIDE - 1,)), dma((SIDE - 1,)), dma((SIDE - 1,)),
        ],
        compiler_params=pltpu.CompilerParams(
            collective_id=0, has_side_effects=True, vmem_limit_bytes=56 << 20
        ),
        cost_estimate=pl.CostEstimate(
            flops=3 * 10**9, bytes_accessed=8 * 10**6, transcendentals=250000
        ),
    )(
        expert_index, gate_weights, tokens, cotangent, w_gate[0], w_up[0], w_down[0]
    )
    return token_grad, down_t.T[None]


def solution(mesh):
    token_spec = P(("dp", "expert"), None)
    weight_spec = P("expert", None, None)
    return jax.shard_map(
        per_device,
        mesh=mesh,
        in_specs=(token_spec,) * 4 + (weight_spec,) * 3,
        out_specs=(token_spec, P("expert", None, "dp")),
        check_vma=False,
    )
```

```python
import functools

import jax
import jax.numpy as jnp
from jax import lax
from jax.experimental import pallas as pl
from jax.experimental.pallas import tpu as pltpu
from jax.sharding import PartitionSpec as P

MESH = pl.DeviceIdType.MESH
F32 = jnp.float32
BF16 = jnp.bfloat16

SIDE = 8
PEERS = 16
SLOTS = 20
MAIN = 16
SPARE = SLOTS - MAIN
FOLD = MAIN // SPARE
GROUP = 4
CHUNKS = PEERS // GROUP
GM = GROUP * MAIN
GS = GROUP * SPARE
GROWS = GM + GS

NT = (((1,), (1,)), ((), ()))
TN = (((0,), (0,)), ((), ()))


def offsets_of(slot):
    pair = slot // 2
    far = 4 - (pair + 1) // 2
    return far * (2 * (pair & 1) - 1), (slot + 1) & 1


def dot(a, b, dims=(((1,), (0,)), ((), ()))):
    return lax.dot_general(a, b, dims, preferred_element_type=F32)


def body(
    ei_ref, gw_ref, tok_hbm, cot_hbm, wg_hbm, wu_hbm, wd_hbm,
    tg_ref, dg_ref,
    tok, cot, wgu, wd, x_out, x_in, c_out, c_in, r_out, r_in,
    t_main, t_spare, xs, pre, scaled, hidden,
    dt_a, dt_b, r_a, r_b, s_a, s_b, q_a, q_b,
    load_sem, xs_sem, xr_sem, cs_sem, cr_sem, rs_sem, rr_sem,
    a1s, a1r, b1s, b1r, a2s, a2r, b2s, b2r,
):
    width = tok.shape[1]
    rows = tok.shape[0]
    ff = wd.shape[0]
    fold = width // FOLD
    part = width // SIDE
    dp = lax.axis_index("dp")
    ex = lax.axis_index("expert")
    z, x = dp // SIDE, dp % SIDE
    y, core = ex // 2, ex % 2

    loads = [
        pltpu.make_async_copy(tok_hbm, tok, load_sem.at[0]),
        pltpu.make_async_copy(cot_hbm, cot, load_sem.at[1]),
        pltpu.make_async_copy(wg_hbm, wgu.at[:, pl.ds(0, ff)], load_sem.at[2]),
        pltpu.make_async_copy(wu_hbm, wgu.at[:, pl.ds(ff, ff)], load_sem.at[3]),
        pltpu.make_async_copy(wd_hbm, wd, load_sem.at[4]),
    ]
    for load in loads:
        load.start()

    def target(slot, way):
        along, other = offsets_of(slot)
        return (dp, ((y + way * along) & (SIDE - 1)) * 2 + ((core + other) & 1))

    def x_peer(k):
        return (z * SIDE + ((x + k) & (SIDE - 1)), ex)

    def z_peer(k):
        return (((z + k) & (SIDE - 1)) * SIDE + x, ex)

    barrier = pltpu.get_barrier_semaphore()
    for slot in range(PEERS - 1):
        pl.semaphore_signal(barrier, inc=1, device_id=target(slot, 1), device_id_type=MESH)
    for k in range(1, SIDE):
        pl.semaphore_signal(barrier, inc=1, device_id=x_peer(k), device_id_type=MESH)
        pl.semaphore_signal(barrier, inc=1, device_id=z_peer(k), device_id_type=MESH)

    sub_e = lax.broadcasted_iota(jnp.int32, (PEERS, rows), 0)
    first = (ei_ref[0:1, :] == sub_e).astype(F32)
    second = (ei_ref[1:2, :] == sub_e).astype(F32)
    chosen = (first + second).astype(BF16)
    gates = gw_ref[...].astype(F32)
    gates = (first * gates[0:1, :] + second * gates[1:2, :]).astype(BF16)
    before = lax.broadcasted_iota(jnp.int32, (rows, rows), 0) < lax.broadcasted_iota(
        jnp.int32, (rows, rows), 1
    )
    place = dot(chosen, before.astype(F32).astype(BF16)).astype(BF16)

    def expert_at(block):
        along, other = offsets_of(block)
        return ((y + along) & (SIDE - 1)) * 2 + ((core + other) & 1)

    nrow = PEERS * MAIN
    down_i = lax.broadcasted_iota(jnp.int32, (nrow, PEERS), 0)
    pick = (
        expert_at(down_i // MAIN) == lax.broadcasted_iota(jnp.int32, (nrow, PEERS), 1)
    ).astype(F32).astype(BF16)
    named = dot(pick, chosen) > 0.5
    at = dot(pick, place).astype(jnp.int32)
    gate_of = dot(pick, gates)
    row_i = lax.broadcasted_iota(jnp.int32, (nrow, rows), 0)
    hit_main = jnp.where(named & (at == (row_i & (MAIN - 1))), 1.0, 0.0)
    hit_spare = jnp.where(named & (at == MAIN + (row_i & (SPARE - 1))), 1.0, 0.0)
    scale_main = jnp.sum(hit_main * gate_of, axis=1, keepdims=True)
    scale_spare = jnp.sum(hit_spare * gate_of, axis=1, keepdims=True)
    piece_i = (row_i & (MAIN - 1)) // SPARE
    take_main = hit_main.astype(BF16)
    take_spare = [
        jnp.where(piece_i == g, hit_spare, 0.0).astype(BF16) for g in range(FOLD)
    ]

    def gather(source, out, scaled_by, lo, hi):
        these = slice(lo * MAIN, hi * MAIN)
        for g in range(FOLD):
            cols = slice(g * fold, (g + 1) * fold)
            got = dot(take_main[these], source[:, cols])
            if scaled_by is not None:
                got = got * scaled_by[0][these]
            out[lo:hi, :, cols] = got.astype(BF16).reshape(hi - lo, MAIN, fold)
        got = dot(take_spare[0][these], source[:, 0:fold])
        for g in range(1, FOLD):
            got = got + dot(take_spare[g][these], source[:, g * fold : (g + 1) * fold])
        if scaled_by is not None:
            got = got * scaled_by[1][these]
        out[lo:hi, :, width:] = got.astype(BF16).reshape(hi - lo, MAIN, fold)

    def move(slot, way, out, into, send, recv):
        return pltpu.make_async_remote_copy(
            src_ref=out.at[slot],
            dst_ref=into.at[slot],
            send_sem=send.at[slot],
            recv_sem=recv.at[slot],
            device_id=target(slot, way),
            device_id_type=MESH,
        )

    own = PEERS - 1
    loads[0].wait()
    gather(tok, x_out, None, 0, GROUP)
    pl.semaphore_wait(barrier, PEERS - 1 + 2 * (SIDE - 1))
    for slot in range(GROUP):
        move(slot, 1, x_out, x_in, xs_sem, xr_sem).start()
    gather(tok, x_out, None, GROUP, PEERS)
    for slot in range(GROUP, PEERS - 1):
        move(slot, 1, x_out, x_in, xs_sem, xr_sem).start()
    loads[1].wait()
    gather(cot, c_out, (scale_main, scale_spare), 0, PEERS)
    for slot in range(PEERS - 1):
        move(slot, 1, c_out, c_in, cs_sem, cr_sem).start()
    x_in[own] = x_out[own]
    c_in[own] = c_out[own]

    pick_t = (
        expert_at(lax.broadcasted_iota(jnp.int32, (PEERS, nrow), 1) // MAIN)
        == lax.broadcasted_iota(jnp.int32, (PEERS, nrow), 0)
    ).astype(F32).astype(BF16)
    named_t = dot(chosen, pick_t, TN) > 0.5
    at_t = dot(place, pick_t, TN).astype(jnp.int32)
    col_i = lax.broadcasted_iota(jnp.int32, (rows, nrow), 1)
    t_main[...] = jnp.where(named_t & (at_t == (col_i & (MAIN - 1))), 1.0, 0.0).astype(BF16)
    t_spare[...] = jnp.where(
        named_t & (at_t == MAIN + (col_i & (SPARE - 1))), 1.0, 0.0
    ).astype(BF16)

    big_i = lax.broadcasted_iota(jnp.int32, (GS, GM), 1)
    small_i = lax.broadcasted_iota(jnp.int32, (GS, GM), 0)
    big_t = lax.broadcasted_iota(jnp.int32, (GM, GS), 0)
    small_t = lax.broadcasted_iota(jnp.int32, (GM, GS), 1)

    def unfold(g):
        want = (small_i // SPARE) * MAIN + g * SPARE + (small_i & (SPARE - 1))
        return jnp.where(big_i == want, 1.0, 0.0).astype(BF16)

    def refold(g):
        want = (small_t // SPARE) * MAIN + g * SPARE + (small_t & (SPARE - 1))
        return jnp.where(big_t == want, 1.0, 0.0).astype(BF16)

    def wait_block(slot, way, out, into, send, recv):
        @pl.when(slot < own)
        def _():
            move(slot, way, out, into, send, recv).wait_recv()

    def unpack(into, chunk, dest, base):
        blocks = into.at[pl.ds(chunk * GROUP, GROUP)]
        dest[pl.ds(base, GM), :] = blocks[:, :, 0:width].reshape(GM, width)
        spare = blocks[:, :, width:].reshape(GM, fold)
        for g in range(FOLD):
            dest[pl.ds(base + GM, GS), pl.ds(g * fold, fold)] = dot(unfold(g), spare).astype(BF16)

    loads[2].wait()
    loads[3].wait()

    def forward(chunk, carry):
        for b in range(GROUP):
            wait_block(chunk * GROUP + b, 1, x_out, x_in, xs_sem, xr_sem)
        base = pl.multiple_of(chunk * GROWS, GROWS)
        unpack(x_in, chunk, xs, 0)
        both = dot(xs[...], wgu[...])
        pre[pl.ds(base, GROWS), :] = both
        gate = both[:, 0:ff]
        hidden[pl.ds(base, GROWS), :] = (gate * jax.nn.sigmoid(gate) * both[:, ff:]).astype(BF16)
        return carry

    lax.fori_loop(0, CHUNKS, forward, 0)
    loads[4].wait()

    def take(chunk, carry):
        for b in range(GROUP):
            wait_block(chunk * GROUP + b, 1, c_out, c_in, cs_sem, cr_sem)
        unpack(c_in, chunk, scaled, pl.multiple_of(chunk * GROWS, GROWS))
        return carry

    def backward(chunk, carry):
        base = pl.multiple_of(chunk * GROWS, GROWS)
        back = dot(scaled[pl.ds(base, GROWS), :], wd[...], NT)
        gate = pre[pl.ds(base, GROWS), 0:ff]
        up = pre[pl.ds(base, GROWS), ff:]
        sig = jax.nn.sigmoid(gate)
        gate_grad = (back * up * sig * (1.0 + gate * (1.0 - sig))).astype(BF16)
        up_grad = (back * (gate * sig)).astype(BF16)
        grads = jnp.concatenate([gate_grad, up_grad], axis=1)
        folded = jnp.zeros((GM, fold), F32)
        for g in range(FOLD):
            cols = pl.ds(g * fold, fold)
            pair = dot(grads, wgu[cols, :], NT).astype(BF16)
            r_out[pl.ds(chunk * GROUP, GROUP), :, cols] = pair[0:GM].reshape(GROUP, MAIN, fold)
            folded = folded + dot(refold(g), pair[GM:])
        r_out[pl.ds(chunk * GROUP, GROUP), :, pl.ds(width, fold)] = folded.astype(BF16).reshape(
            GROUP, MAIN, fold
        )
        for b in range(GROUP):
            slot = chunk * GROUP + b

            @pl.when(slot < own)
            def _():
                move(slot, -1, r_out, r_in, rs_sem, rr_sem).start()

        return carry

    def both_steps(chunk, carry):
        return backward(chunk, take(chunk, carry))

    half = part // (2 * SIDE)

    def share(k, peer, at_axis, out, into, send, recv):
        return pltpu.make_async_remote_copy(
            src_ref=out.at[(at_axis + k) & (SIDE - 1)],
            dst_ref=into.at[k - 1],
            send_sem=send.at[k - 1],
            recv_sem=recv.at[k - 1],
            device_id=peer(k),
            device_id_type=MESH,
        )

    def outer(step, carry):
        k = (4 - (step + 1) // 2) * (2 * (step & 1) - 1) & (SIDE - 1)
        zz = (z + k) & (SIDE - 1)
        cols = pl.ds(pl.multiple_of(zz * part, part), part)
        term = dot(scaled[:, cols], hidden[...], TN).astype(BF16).reshape(SIDE, 2, half, ff)
        for xx in range(SIDE):
            dt_a[xx, zz] = term[xx, 0]
        dt_b[zz] = term[:, 1]

        @pl.when(step < SIDE - 1)
        def _():
            share(k, z_peer, z, dt_b, r_b, b1s, b1r).start()

        return carry

    order = (4, 3, 5, 2, 6, 1, 7)
    lax.fori_loop(0, CHUNKS // 2, both_steps, 0)
    lax.fori_loop(CHUNKS // 2, CHUNKS, take, 0)
    lax.fori_loop(0, SIDE, outer, 0)
    for k in order:
        share(k, x_peer, x, dt_a, r_a, a1s, a1r).start()
    lax.fori_loop(CHUNKS // 2, CHUNKS, backward, 0)
    r_in[own] = r_out[own]

    for k in order:
        share(k, x_peer, x, dt_a, r_a, a1s, a1r).wait_recv()
    total = dt_a[x].astype(F32)
    for k in range(SIDE - 1):
        total = total + r_a[k].astype(F32)
    s_a[...] = total.astype(BF16)
    for k in order:
        share(k, z_peer, z, s_a, q_a, a2s, a2r).start()
    for k in order:
        share(k, z_peer, z, dt_b, r_b, b1s, b1r).wait_recv()
    total = dt_b[z].astype(F32)
    for k in range(SIDE - 1):
        total = total + r_b[k].astype(F32)
    s_b[...] = total.astype(BF16)
    for k in order:
        share(k, x_peer, x, s_b, q_b, b2s, b2r).start()
    for k in order:
        share(k, z_peer, z, s_a, q_a, a2s, a2r).wait_recv()
        share(k, x_peer, x, s_b, q_b, b2s, b2r).wait_recv()
    total = s_a[z].astype(F32)
    for k in range(SIDE - 1):
        total = total + q_a[k].astype(F32)
    dg_ref[0:half, :] = total
    total = s_b[x].astype(F32)
    for k in range(SIDE - 1):
        total = total + q_b[k].astype(F32)
    dg_ref[half:, :] = total

    for slot in range(PEERS - 1):
        move(slot, 1, x_out, x_in, xs_sem, xr_sem).wait_send()
        move(slot, 1, c_out, c_in, cs_sem, cr_sem).wait_send()
    for k in order:
        share(k, x_peer, x, dt_a, r_a, a1s, a1r).wait_send()
        share(k, z_peer, z, dt_b, r_b, b1s, b1r).wait_send()
        share(k, z_peer, z, s_a, q_a, a2s, a2r).wait_send()
        share(k, x_peer, x, s_b, q_b, b2s, b2r).wait_send()
    for slot in range(PEERS - 1):
        move(slot, -1, r_out, r_in, rs_sem, rr_sem).wait_recv()
    col_piece = (lax.broadcasted_iota(jnp.int32, (rows, nrow), 1) & (MAIN - 1)) // SPARE
    spare = r_in[:, :, width:].reshape(nrow, fold)
    for g in range(FOLD):
        cols = slice(g * fold, (g + 1) * fold)
        main = r_in[:, :, cols].reshape(nrow, fold)
        pick_g = jnp.where(col_piece == g, t_spare[...].astype(F32), 0.0).astype(BF16)
        tg_ref[:, cols] = (dot(t_main[...], main) + dot(pick_g, spare)).astype(BF16)

    for slot in range(PEERS - 1):
        move(slot, -1, r_out, r_in, rs_sem, rr_sem).wait_send()


def hand_over(tg_in, dg_in, tg_ref, dg_ref, sem):
    copies = [
        pltpu.make_async_copy(tg_in, tg_ref, sem.at[0]),
        pltpu.make_async_copy(dg_in, dg_ref, sem.at[1]),
    ]
    for copy in copies:
        copy.start()
    for copy in copies:
        copy.wait()


def per_device(tokens, expert_index, gate_weights, cotangent, w_gate, w_up, w_down):
    rows, width = tokens.shape
    ff = w_gate.shape[2]
    wide = width + width // FOLD
    half = width // (2 * SIDE * SIDE)
    vmem = pl.BlockSpec(memory_space=pltpu.VMEM)
    hbm = pl.BlockSpec(memory_space=pl.ANY)
    blocks = pltpu.VMEM((PEERS, MAIN, wide), BF16)
    dma = pltpu.SemaphoreType.DMA
    token_grad, down_t = pl.pallas_call(
        body,
        out_shape=(
            jax.ShapeDtypeStruct((rows, width), BF16),
            jax.ShapeDtypeStruct((2 * half, ff), F32),
        ),
        in_specs=[vmem, vmem, hbm, hbm, hbm, hbm, hbm],
        out_specs=(vmem, vmem),
        scratch_shapes=[
            pltpu.VMEM((rows, width), BF16),
            pltpu.VMEM((rows, width), BF16),
            pltpu.VMEM((width, 2 * ff), BF16),
            pltpu.VMEM((ff, width), BF16),
            blocks, blocks, blocks, blocks, blocks, blocks,
            pltpu.VMEM((rows, PEERS * MAIN), BF16),
            pltpu.VMEM((rows, PEERS * MAIN), BF16),
            pltpu.VMEM((GROWS, width), BF16),
            pltpu.VMEM((CHUNKS * GROWS, 2 * ff), F32),
            pltpu.VMEM((CHUNKS * GROWS, width), BF16),
            pltpu.VMEM((CHUNKS * GROWS, ff), BF16),
            pltpu.VMEM((SIDE, SIDE, half, ff), BF16),
            pltpu.VMEM((SIDE, SIDE, half, ff), BF16),
            pltpu.VMEM((SIDE - 1, SIDE, half, ff), BF16),
            pltpu.VMEM((SIDE - 1, SIDE, half, ff), BF16),
            pltpu.VMEM((SIDE, half, ff), BF16),
            pltpu.VMEM((SIDE, half, ff), BF16),
            pltpu.VMEM((SIDE - 1, half, ff), BF16),
            pltpu.VMEM((SIDE - 1, half, ff), BF16),
            dma((5,)),
            dma((PEERS,)), dma((PEERS,)), dma((PEERS,)), dma((PEERS,)), dma((PEERS,)), dma((PEERS,)),
            dma((SIDE - 1,)), dma((SIDE - 1,)), dma((SIDE - 1,)), dma((SIDE - 1,)),
            dma((SIDE - 1,)), dma((SIDE - 1,)), dma((SIDE - 1,)), dma((SIDE - 1,)),
        ],
        compiler_params=pltpu.CompilerParams(
            collective_id=0, has_side_effects=True, vmem_limit_bytes=56 << 20
        ),
        cost_estimate=pl.CostEstimate(
            flops=3 * 10**9, bytes_accessed=8 * 10**6, transcendentals=250000
        ),
    )(
        expert_index.T, gate_weights.T, tokens, cotangent, w_gate[0], w_up[0], w_down[0]
    )
    token_grad, down_t = pl.pallas_call(
        hand_over,
        out_shape=(
            jax.ShapeDtypeStruct((rows, width), BF16),
            jax.ShapeDtypeStruct((2 * half, ff), F32),
        ),
        in_specs=[vmem, vmem],
        out_specs=(hbm, hbm),
        scratch_shapes=[dma((2,))],
    )(token_grad, down_t)
    return token_grad, down_t.T[None]


def solution(mesh):
    token_spec = P(("dp", "expert"), None)
    weight_spec = P("expert", None, None)
    return jax.shard_map(
        per_device,
        mesh=mesh,
        in_specs=(token_spec,) * 4 + (weight_spec,) * 3,
        out_specs=(token_spec, P("expert", None, "dp")),
        check_vma=False,
    )
```

```python
import functools

import jax
import jax.numpy as jnp
from jax import lax
from jax.experimental import pallas as pl
from jax.experimental.pallas import tpu as pltpu
from jax.sharding import PartitionSpec as P

MESH = pl.DeviceIdType.MESH
F32 = jnp.float32
BF16 = jnp.bfloat16

SIDE = 8
PEERS = 16
SLOTS = 20
MAIN = 16
SPARE = SLOTS - MAIN
FOLD = MAIN // SPARE
GROUP = 4
CHUNKS = PEERS // GROUP
NEWS = 1
GM = GROUP * MAIN
GS = GROUP * SPARE
GROWS = GM + GS

NT = (((1,), (1,)), ((), ()))
TN = (((0,), (0,)), ((), ()))


def offsets_of(slot):
    pair = slot // 2
    far = 4 - (pair + 1) // 2
    return far * (2 * (pair & 1) - 1), (slot + 1) & 1


def dot(a, b, dims=(((1,), (0,)), ((), ()))):
    return lax.dot_general(a, b, dims, preferred_element_type=F32)


def body(
    ei_ref, gw_ref, tok_hbm, cot_hbm, wg_hbm, wu_hbm, wd_hbm,
    tg_ref, dg_ref,
    tok, cot, wgu, wd, x_out, x_in, c_out, c_in, r_out, r_in,
    t_main, t_spare, xs, pre, scaled, hidden,
    dt_a, dt_b, r_a, r_b, s_a, s_b, q_a, q_b,
    load_sem, xs_sem, xr_sem, cs_sem, cr_sem, rs_sem, rr_sem,
    a1s, a1r, b1s, b1r, a2s, a2r, b2s, b2r, ring_go, dp_go,
):
    width = tok.shape[1]
    rows = tok.shape[0]
    ff = wd.shape[0]
    fold = width // FOLD
    part = width // SIDE
    dp = lax.axis_index("dp")
    ex = lax.axis_index("expert")
    z, x = dp // SIDE, dp % SIDE
    y, core = ex // 2, ex % 2

    loads = [
        pltpu.make_async_copy(tok_hbm, tok, load_sem.at[0]),
        pltpu.make_async_copy(cot_hbm, cot, load_sem.at[1]),
        pltpu.make_async_copy(wg_hbm, wgu.at[:, pl.ds(0, ff)], load_sem.at[2]),
        pltpu.make_async_copy(wu_hbm, wgu.at[:, pl.ds(ff, ff)], load_sem.at[3]),
        pltpu.make_async_copy(wd_hbm, wd, load_sem.at[4]),
    ]
    for load in loads:
        load.start()

    def target(slot, way):
        along, other = offsets_of(slot)
        return (dp, ((y + way * along) & (SIDE - 1)) * 2 + ((core + other) & 1))

    def x_peer(k):
        return (z * SIDE + ((x + k) & (SIDE - 1)), ex)

    def z_peer(k):
        return (((z + k) & (SIDE - 1)) * SIDE + x, ex)

    barrier = pltpu.get_barrier_semaphore()
    for e in range(PEERS):
        if e != NEWS:

            @pl.when(ex != e)
            def _():
                pl.semaphore_signal(barrier, inc=1, device_id=(dp, e), device_id_type=MESH)

    sub_e = lax.broadcasted_iota(jnp.int32, (PEERS, rows), 0)
    first = (ei_ref[0:1, :] == sub_e).astype(F32)
    second = (ei_ref[1:2, :] == sub_e).astype(F32)
    chosen = (first + second).astype(BF16)
    gates = gw_ref[...].astype(F32)
    gates = (first * gates[0:1, :] + second * gates[1:2, :]).astype(BF16)
    before = lax.broadcasted_iota(jnp.int32, (rows, rows), 0) < lax.broadcasted_iota(
        jnp.int32, (rows, rows), 1
    )
    place = dot(chosen, before.astype(F32).astype(BF16)).astype(BF16)

    def expert_at(block):
        along, other = offsets_of(block)
        return ((y + along) & (SIDE - 1)) * 2 + ((core + other) & 1)

    nrow = PEERS * MAIN
    down_i = lax.broadcasted_iota(jnp.int32, (nrow, PEERS), 0)
    pick = (
        expert_at(down_i // MAIN) == lax.broadcasted_iota(jnp.int32, (nrow, PEERS), 1)
    ).astype(F32).astype(BF16)
    named = dot(pick, chosen) > 0.5
    at = dot(pick, place).astype(jnp.int32)
    gate_of = dot(pick, gates)
    row_i = lax.broadcasted_iota(jnp.int32, (nrow, rows), 0)
    hit_main = jnp.where(named & (at == (row_i & (MAIN - 1))), 1.0, 0.0)
    hit_spare = jnp.where(named & (at == MAIN + (row_i & (SPARE - 1))), 1.0, 0.0)
    scale_main = jnp.sum(hit_main * gate_of, axis=1, keepdims=True)
    scale_spare = jnp.sum(hit_spare * gate_of, axis=1, keepdims=True)
    piece_i = (row_i & (MAIN - 1)) // SPARE
    take_main = hit_main.astype(BF16)
    take_spare = [
        jnp.where(piece_i == g, hit_spare, 0.0).astype(BF16) for g in range(FOLD)
    ]

    def gather(source, out, scaled_by, lo, hi):
        these = slice(lo * MAIN, hi * MAIN)
        for g in range(FOLD):
            cols = slice(g * fold, (g + 1) * fold)
            got = dot(take_main[these], source[:, cols])
            if scaled_by is not None:
                got = got * scaled_by[0][these]
            out[lo:hi, :, cols] = got.astype(BF16).reshape(hi - lo, MAIN, fold)
        got = dot(take_spare[0][these], source[:, 0:fold])
        for g in range(1, FOLD):
            got = got + dot(take_spare[g][these], source[:, g * fold : (g + 1) * fold])
        if scaled_by is not None:
            got = got * scaled_by[1][these]
        out[lo:hi, :, width:] = got.astype(BF16).reshape(hi - lo, MAIN, fold)

    def move(slot, way, out, into, send, recv):
        return pltpu.make_async_remote_copy(
            src_ref=out.at[slot],
            dst_ref=into.at[slot],
            send_sem=send.at[slot],
            recv_sem=recv.at[slot],
            device_id=target(slot, way),
            device_id_type=MESH,
        )

    own = PEERS - 1

    loads[0].wait()
    gather(tok, x_out, None, 0, GROUP)

    @pl.when(ex != NEWS)
    def _():
        pl.semaphore_wait(barrier, PEERS - 1)

    @pl.when(ex == 0)
    def _():
        pl.semaphore_signal(ring_go, inc=1, device_id=(dp, NEWS), device_id_type=MESH)

    @pl.when(ex == NEWS)
    def _():
        pl.semaphore_wait(ring_go, 1)

    for slot in range(GROUP):
        move(slot, 1, x_out, x_in, xs_sem, xr_sem).start()
    gather(tok, x_out, None, GROUP, PEERS)
    for slot in range(GROUP, PEERS - 1):
        move(slot, 1, x_out, x_in, xs_sem, xr_sem).start()

    @pl.when(ex == NEWS)
    def _():
        for k in range(1, SIDE):
            pl.semaphore_signal(barrier, inc=1, device_id=x_peer(k), device_id_type=MESH)
            pl.semaphore_signal(barrier, inc=1, device_id=z_peer(k), device_id_type=MESH)

    loads[1].wait()
    gather(cot, c_out, (scale_main, scale_spare), 0, PEERS)
    for slot in range(PEERS - 1):
        move(slot, 1, c_out, c_in, cs_sem, cr_sem).start()
    x_in[own] = x_out[own]
    c_in[own] = c_out[own]

    pick_t = (
        expert_at(lax.broadcasted_iota(jnp.int32, (PEERS, nrow), 1) // MAIN)
        == lax.broadcasted_iota(jnp.int32, (PEERS, nrow), 0)
    ).astype(F32).astype(BF16)
    named_t = dot(chosen, pick_t, TN) > 0.5
    at_t = dot(place, pick_t, TN).astype(jnp.int32)
    col_i = lax.broadcasted_iota(jnp.int32, (rows, nrow), 1)
    t_main[...] = jnp.where(named_t & (at_t == (col_i & (MAIN - 1))), 1.0, 0.0).astype(BF16)
    t_spare[...] = jnp.where(
        named_t & (at_t == MAIN + (col_i & (SPARE - 1))), 1.0, 0.0
    ).astype(BF16)

    big_i = lax.broadcasted_iota(jnp.int32, (GS, GM), 1)
    small_i = lax.broadcasted_iota(jnp.int32, (GS, GM), 0)
    big_t = lax.broadcasted_iota(jnp.int32, (GM, GS), 0)
    small_t = lax.broadcasted_iota(jnp.int32, (GM, GS), 1)

    def unfold(g):
        want = (small_i // SPARE) * MAIN + g * SPARE + (small_i & (SPARE - 1))
        return jnp.where(big_i == want, 1.0, 0.0).astype(BF16)

    def refold(g):
        want = (small_t // SPARE) * MAIN + g * SPARE + (small_t & (SPARE - 1))
        return jnp.where(big_t == want, 1.0, 0.0).astype(BF16)

    def wait_block(slot, way, out, into, send, recv):
        @pl.when(slot < own)
        def _():
            move(slot, way, out, into, send, recv).wait_recv()

    def unpack(into, chunk, dest, base):
        blocks = into.at[pl.ds(chunk * GROUP, GROUP)]
        dest[pl.ds(base, GM), :] = blocks[:, :, 0:width].reshape(GM, width)
        spare = blocks[:, :, width:].reshape(GM, fold)
        for g in range(FOLD):
            dest[pl.ds(base + GM, GS), pl.ds(g * fold, fold)] = dot(unfold(g), spare).astype(BF16)

    loads[2].wait()
    loads[3].wait()

    def forward(chunk, carry):
        for b in range(GROUP):
            wait_block(chunk * GROUP + b, 1, x_out, x_in, xs_sem, xr_sem)
        base = pl.multiple_of(chunk * GROWS, GROWS)
        unpack(x_in, chunk, xs, 0)
        both = dot(xs[...], wgu[...])
        pre[pl.ds(base, GROWS), :] = both
        gate = both[:, 0:ff]
        hidden[pl.ds(base, GROWS), :] = (gate * jax.nn.sigmoid(gate) * both[:, ff:]).astype(BF16)
        return carry

    lax.fori_loop(0, CHUNKS, forward, 0)

    @pl.when(ex == NEWS)
    def _():
        pl.semaphore_wait(barrier, 2 * (SIDE - 1))
        for e in range(PEERS):
            if e != NEWS:
                pl.semaphore_signal(dp_go, inc=1, device_id=(dp, e), device_id_type=MESH)

    loads[4].wait()

    def take(chunk, carry):
        for b in range(GROUP):
            wait_block(chunk * GROUP + b, 1, c_out, c_in, cs_sem, cr_sem)
        unpack(c_in, chunk, scaled, pl.multiple_of(chunk * GROWS, GROWS))
        return carry

    def backward(chunk, carry):
        base = pl.multiple_of(chunk * GROWS, GROWS)
        back = dot(scaled[pl.ds(base, GROWS), :], wd[...], NT)
        gate = pre[pl.ds(base, GROWS), 0:ff]
        up = pre[pl.ds(base, GROWS), ff:]
        sig = jax.nn.sigmoid(gate)
        gate_grad = (back * up * sig * (1.0 + gate * (1.0 - sig))).astype(BF16)
        up_grad = (back * (gate * sig)).astype(BF16)
        grads = jnp.concatenate([gate_grad, up_grad], axis=1)
        folded = jnp.zeros((GM, fold), F32)
        for g in range(FOLD):
            cols = pl.ds(g * fold, fold)
            pair = dot(grads, wgu[cols, :], NT).astype(BF16)
            r_out[pl.ds(chunk * GROUP, GROUP), :, cols] = pair[0:GM].reshape(GROUP, MAIN, fold)
            folded = folded + dot(refold(g), pair[GM:])
        r_out[pl.ds(chunk * GROUP, GROUP), :, pl.ds(width, fold)] = folded.astype(BF16).reshape(
            GROUP, MAIN, fold
        )
        return carry

    def send_back(chunk, carry):
        for b in range(GROUP):
            slot = chunk * GROUP + b

            @pl.when(slot < own)
            def _():
                move(slot, -1, r_out, r_in, rs_sem, rr_sem).start()

        return carry

    def both_steps(chunk, carry):
        return backward(chunk, take(chunk, carry))

    half = part // (2 * SIDE)

    def share(k, peer, at_axis, out, into, send, recv):
        return pltpu.make_async_remote_copy(
            src_ref=out.at[(at_axis + k) & (SIDE - 1)],
            dst_ref=into.at[k - 1],
            send_sem=send.at[k - 1],
            recv_sem=recv.at[k - 1],
            device_id=peer(k),
            device_id_type=MESH,
        )

    def outer(step, carry):
        k = (4 - (step + 1) // 2) * (2 * (step & 1) - 1) & (SIDE - 1)
        zz = (z + k) & (SIDE - 1)
        cols = pl.ds(pl.multiple_of(zz * part, part), part)
        term = dot(scaled[:, cols], hidden[...], TN).astype(BF16).reshape(SIDE, 2, half, ff)
        for xx in range(SIDE):
            dt_a[xx, zz] = term[xx, 0]
        dt_b[zz] = term[:, 1]

        @pl.when(step < SIDE - 1)
        def _():
            share(k, z_peer, z, dt_b, r_b, b1s, b1r).start()

        return carry

    order = (4, 3, 5, 2, 6, 1, 7)
    lax.fori_loop(0, CHUNKS // 2, both_steps, 0)
    lax.fori_loop(CHUNKS // 2, CHUNKS, take, 0)
    lax.fori_loop(0, CHUNKS // 2, send_back, 0)

    @pl.when(ex != NEWS)
    def _():
        pl.semaphore_wait(dp_go, 1)

    lax.fori_loop(0, SIDE, outer, 0)
    for k in order:
        share(k, x_peer, x, dt_a, r_a, a1s, a1r).start()
    lax.fori_loop(
        CHUNKS // 2, CHUNKS, lambda chunk, carry: send_back(chunk, backward(chunk, carry)), 0
    )
    r_in[own] = r_out[own]

    for k in order:
        share(k, x_peer, x, dt_a, r_a, a1s, a1r).wait_recv()
    total = dt_a[x].astype(F32)
    for k in range(SIDE - 1):
        total = total + r_a[k].astype(F32)
    s_a[...] = total.astype(BF16)
    for k in order:
        share(k, z_peer, z, s_a, q_a, a2s, a2r).start()
    for k in order:
        share(k, z_peer, z, dt_b, r_b, b1s, b1r).wait_recv()
    total = dt_b[z].astype(F32)
    for k in range(SIDE - 1):
        total = total + r_b[k].astype(F32)
    s_b[...] = total.astype(BF16)
    for k in order:
        share(k, x_peer, x, s_b, q_b, b2s, b2r).start()
    for slot in range(PEERS - 1):
        move(slot, 1, x_out, x_in, xs_sem, xr_sem).wait_send()
        move(slot, 1, c_out, c_in, cs_sem, cr_sem).wait_send()
    for slot in range(PEERS - 1):
        move(slot, -1, r_out, r_in, rs_sem, rr_sem).wait_recv()
    col_piece = (lax.broadcasted_iota(jnp.int32, (rows, nrow), 1) & (MAIN - 1)) // SPARE
    spare = r_in[:, :, width:].reshape(nrow, fold)
    for g in range(FOLD):
        cols = slice(g * fold, (g + 1) * fold)
        main = r_in[:, :, cols].reshape(nrow, fold)
        pick_g = jnp.where(col_piece == g, t_spare[...].astype(F32), 0.0).astype(BF16)
        tg_ref[:, cols] = (dot(t_main[...], main) + dot(pick_g, spare)).astype(BF16)

    for k in order:
        share(k, z_peer, z, s_a, q_a, a2s, a2r).wait_recv()
        share(k, x_peer, x, s_b, q_b, b2s, b2r).wait_recv()
    total = s_a[z].astype(F32)
    for k in range(SIDE - 1):
        total = total + q_a[k].astype(F32)
    dg_ref[0:half, :] = total
    total = s_b[x].astype(F32)
    for k in range(SIDE - 1):
        total = total + q_b[k].astype(F32)
    dg_ref[half:, :] = total

    for k in order:
        share(k, x_peer, x, dt_a, r_a, a1s, a1r).wait_send()
        share(k, z_peer, z, dt_b, r_b, b1s, b1r).wait_send()
        share(k, z_peer, z, s_a, q_a, a2s, a2r).wait_send()
        share(k, x_peer, x, s_b, q_b, b2s, b2r).wait_send()
    for slot in range(PEERS - 1):
        move(slot, -1, r_out, r_in, rs_sem, rr_sem).wait_send()


def hand_over(tg_in, dg_in, tg_ref, dg_ref, sem):
    copies = [
        pltpu.make_async_copy(tg_in, tg_ref, sem.at[0]),
        pltpu.make_async_copy(dg_in, dg_ref, sem.at[1]),
    ]
    for copy in copies:
        copy.start()
    for copy in copies:
        copy.wait()


def per_device(tokens, expert_index, gate_weights, cotangent, w_gate, w_up, w_down):
    rows, width = tokens.shape
    ff = w_gate.shape[2]
    wide = width + width // FOLD
    half = width // (2 * SIDE * SIDE)
    vmem = pl.BlockSpec(memory_space=pltpu.VMEM)
    hbm = pl.BlockSpec(memory_space=pl.ANY)
    blocks = pltpu.VMEM((PEERS, MAIN, wide), BF16)
    dma = pltpu.SemaphoreType.DMA
    token_grad, down_t = pl.pallas_call(
        body,
        out_shape=(
            jax.ShapeDtypeStruct((rows, width), BF16),
            jax.ShapeDtypeStruct((2 * half, ff), F32),
        ),
        in_specs=[vmem, vmem, hbm, hbm, hbm, hbm, hbm],
        out_specs=(vmem, vmem),
        scratch_shapes=[
            pltpu.VMEM((rows, width), BF16),
            pltpu.VMEM((rows, width), BF16),
            pltpu.VMEM((width, 2 * ff), BF16),
            pltpu.VMEM((ff, width), BF16),
            blocks, blocks, blocks, blocks, blocks, blocks,
            pltpu.VMEM((rows, PEERS * MAIN), BF16),
            pltpu.VMEM((rows, PEERS * MAIN), BF16),
            pltpu.VMEM((GROWS, width), BF16),
            pltpu.VMEM((CHUNKS * GROWS, 2 * ff), F32),
            pltpu.VMEM((CHUNKS * GROWS, width), BF16),
            pltpu.VMEM((CHUNKS * GROWS, ff), BF16),
            pltpu.VMEM((SIDE, SIDE, half, ff), BF16),
            pltpu.VMEM((SIDE, SIDE, half, ff), BF16),
            pltpu.VMEM((SIDE - 1, SIDE, half, ff), BF16),
            pltpu.VMEM((SIDE - 1, SIDE, half, ff), BF16),
            pltpu.VMEM((SIDE, half, ff), BF16),
            pltpu.VMEM((SIDE, half, ff), BF16),
            pltpu.VMEM((SIDE - 1, half, ff), BF16),
            pltpu.VMEM((SIDE - 1, half, ff), BF16),
            dma((5,)),
            dma((PEERS,)), dma((PEERS,)), dma((PEERS,)), dma((PEERS,)), dma((PEERS,)), dma((PEERS,)),
            dma((SIDE - 1,)), dma((SIDE - 1,)), dma((SIDE - 1,)), dma((SIDE - 1,)),
            dma((SIDE - 1,)), dma((SIDE - 1,)), dma((SIDE - 1,)), dma((SIDE - 1,)),
            pltpu.SemaphoreType.REGULAR, pltpu.SemaphoreType.REGULAR,
        ],
        compiler_params=pltpu.CompilerParams(
            collective_id=0, has_side_effects=True, vmem_limit_bytes=56 << 20
        ),
        cost_estimate=pl.CostEstimate(
            flops=3 * 10**9, bytes_accessed=8 * 10**6, transcendentals=250000
        ),
    )(
        expert_index.T, gate_weights.T, tokens, cotangent, w_gate[0], w_up[0], w_down[0]
    )
    token_grad, down_t = pl.pallas_call(
        hand_over,
        out_shape=(
            jax.ShapeDtypeStruct((rows, width), BF16),
            jax.ShapeDtypeStruct((2 * half, ff), F32),
        ),
        in_specs=[vmem, vmem],
        out_specs=(hbm, hbm),
        scratch_shapes=[dma((2,))],
    )(token_grad, down_t)
    return token_grad, down_t.T[None]


def solution(mesh):
    token_spec = P(("dp", "expert"), None)
    weight_spec = P("expert", None, None)
    return jax.shard_map(
        per_device,
        mesh=mesh,
        in_specs=(token_spec,) * 4 + (weight_spec,) * 3,
        out_specs=(token_spec, P("expert", None, "dp")),
        check_vma=False,
    )
```

```python
import functools

import jax
import jax.numpy as jnp
from jax import lax
from jax.experimental import pallas as pl
from jax.experimental.pallas import tpu as pltpu
from jax.sharding import PartitionSpec as P

MESH = pl.DeviceIdType.MESH
F32 = jnp.float32
BF16 = jnp.bfloat16

SIDE = 8
PEERS = 16
SLOTS = 20
MAIN = 16
SPARE = SLOTS - MAIN
FOLD = MAIN // SPARE
GROUP = 4
CHUNKS = PEERS // GROUP
NEWS = 1
GM = GROUP * MAIN
GS = GROUP * SPARE
GROWS = GM + GS

NT = (((1,), (1,)), ((), ()))
TN = (((0,), (0,)), ((), ()))


def offsets_of(slot):
    pair = slot // 2
    far = 4 - (pair + 1) // 2
    return far * (2 * (pair & 1) - 1), (slot + 1) & 1


def dot(a, b, dims=(((1,), (0,)), ((), ()))):
    return lax.dot_general(a, b, dims, preferred_element_type=F32)


def body(
    ei_ref, gw_ref, tok_hbm, cot_hbm, wg_hbm, wu_hbm, wd_hbm,
    tg_ref, dg_ref,
    tok, cot, wgu, wd, x_out, x_in, c_out, c_in, r_out, r_in,
    t_main, t_spare, xs, pre, scaled, hidden,
    dt_a, dt_b, r_a, r_b, s_a, s_b, q_a, q_b,
    load_sem, xs_sem, xr_sem, cs_sem, cr_sem, rs_sem, rr_sem,
    a1s, a1r, b1s, b1r, a2s, a2r, b2s, b2r, ring_go, dp_go, tg_out, leave_sem,
):
    width = tok.shape[1]
    rows = tok.shape[0]
    ff = wd.shape[0]
    fold = width // FOLD
    part = width // SIDE
    dp = lax.axis_index("dp")
    ex = lax.axis_index("expert")
    z, x = dp // SIDE, dp % SIDE
    y, core = ex // 2, ex % 2

    loads = [
        pltpu.make_async_copy(tok_hbm, tok, load_sem.at[0]),
        pltpu.make_async_copy(cot_hbm, cot, load_sem.at[1]),
        pltpu.make_async_copy(wg_hbm, wgu.at[:, pl.ds(0, ff)], load_sem.at[2]),
        pltpu.make_async_copy(wu_hbm, wgu.at[:, pl.ds(ff, ff)], load_sem.at[3]),
        pltpu.make_async_copy(wd_hbm, wd, load_sem.at[4]),
    ]
    for load in loads:
        load.start()

    def target(slot, way):
        along, other = offsets_of(slot)
        return (dp, ((y + way * along) & (SIDE - 1)) * 2 + ((core + other) & 1))

    def x_peer(k):
        return (z * SIDE + ((x + k) & (SIDE - 1)), ex)

    def z_peer(k):
        return (((z + k) & (SIDE - 1)) * SIDE + x, ex)

    barrier = pltpu.get_barrier_semaphore()
    for e in range(PEERS):
        if e != NEWS:

            @pl.when(ex != e)
            def _():
                pl.semaphore_signal(barrier, inc=1, device_id=(dp, e), device_id_type=MESH)

    sub_e = lax.broadcasted_iota(jnp.int32, (PEERS, rows), 0)
    first = (ei_ref[0:1, :] == sub_e).astype(F32)
    second = (ei_ref[1:2, :] == sub_e).astype(F32)
    chosen = (first + second).astype(BF16)
    gates = gw_ref[...].astype(F32)
    gates = (first * gates[0:1, :] + second * gates[1:2, :]).astype(BF16)
    before = lax.broadcasted_iota(jnp.int32, (rows, rows), 0) < lax.broadcasted_iota(
        jnp.int32, (rows, rows), 1
    )
    place = dot(chosen, before.astype(F32).astype(BF16)).astype(BF16)

    def expert_at(block):
        along, other = offsets_of(block)
        return ((y + along) & (SIDE - 1)) * 2 + ((core + other) & 1)

    nrow = PEERS * MAIN
    down_i = lax.broadcasted_iota(jnp.int32, (nrow, PEERS), 0)
    pick = (
        expert_at(down_i // MAIN) == lax.broadcasted_iota(jnp.int32, (nrow, PEERS), 1)
    ).astype(F32).astype(BF16)
    named = dot(pick, chosen) > 0.5
    at = dot(pick, place).astype(jnp.int32)
    gate_of = dot(pick, gates)
    row_i = lax.broadcasted_iota(jnp.int32, (nrow, rows), 0)
    hit_main = jnp.where(named & (at == (row_i & (MAIN - 1))), 1.0, 0.0)
    hit_spare = jnp.where(named & (at == MAIN + (row_i & (SPARE - 1))), 1.0, 0.0)
    scale_main = jnp.sum(hit_main * gate_of, axis=1, keepdims=True)
    scale_spare = jnp.sum(hit_spare * gate_of, axis=1, keepdims=True)
    piece_i = (row_i & (MAIN - 1)) // SPARE
    take_main = hit_main.astype(BF16)
    take_spare = [
        jnp.where(piece_i == g, hit_spare, 0.0).astype(BF16) for g in range(FOLD)
    ]

    def gather(source, out, scaled_by, lo, hi):
        these = slice(lo * MAIN, hi * MAIN)
        for g in range(FOLD):
            cols = slice(g * fold, (g + 1) * fold)
            got = dot(take_main[these], source[:, cols])
            if scaled_by is not None:
                got = got * scaled_by[0][these]
            out[lo:hi, :, cols] = got.astype(BF16).reshape(hi - lo, MAIN, fold)
        got = dot(take_spare[0][these], source[:, 0:fold])
        for g in range(1, FOLD):
            got = got + dot(take_spare[g][these], source[:, g * fold : (g + 1) * fold])
        if scaled_by is not None:
            got = got * scaled_by[1][these]
        out[lo:hi, :, width:] = got.astype(BF16).reshape(hi - lo, MAIN, fold)

    def move(slot, way, out, into, send, recv):
        return pltpu.make_async_remote_copy(
            src_ref=out.at[slot],
            dst_ref=into.at[slot],
            send_sem=send.at[slot],
            recv_sem=recv.at[slot],
            device_id=target(slot, way),
            device_id_type=MESH,
        )

    own = PEERS - 1

    loads[0].wait()
    gather(tok, x_out, None, 0, GROUP)

    @pl.when(ex != NEWS)
    def _():
        pl.semaphore_wait(barrier, PEERS - 1)

    @pl.when(ex == 0)
    def _():
        pl.semaphore_signal(ring_go, inc=1, device_id=(dp, NEWS), device_id_type=MESH)

    @pl.when(ex == NEWS)
    def _():
        pl.semaphore_wait(ring_go, 1)

    for slot in range(GROUP):
        move(slot, 1, x_out, x_in, xs_sem, xr_sem).start()
    gather(tok, x_out, None, GROUP, PEERS)
    for slot in range(GROUP, PEERS - 1):
        move(slot, 1, x_out, x_in, xs_sem, xr_sem).start()

    @pl.when(ex == NEWS)
    def _():
        for k in range(1, SIDE):
            pl.semaphore_signal(barrier, inc=1, device_id=x_peer(k), device_id_type=MESH)
            pl.semaphore_signal(barrier, inc=1, device_id=z_peer(k), device_id_type=MESH)

    loads[1].wait()
    gather(cot, c_out, (scale_main, scale_spare), 0, PEERS)
    for slot in range(PEERS - 1):
        move(slot, 1, c_out, c_in, cs_sem, cr_sem).start()
    x_in[own] = x_out[own]
    c_in[own] = c_out[own]

    pick_t = (
        expert_at(lax.broadcasted_iota(jnp.int32, (PEERS, nrow), 1) // MAIN)
        == lax.broadcasted_iota(jnp.int32, (PEERS, nrow), 0)
    ).astype(F32).astype(BF16)
    named_t = dot(chosen, pick_t, TN) > 0.5
    at_t = dot(place, pick_t, TN).astype(jnp.int32)
    col_i = lax.broadcasted_iota(jnp.int32, (rows, nrow), 1)
    t_main[...] = jnp.where(named_t & (at_t == (col_i & (MAIN - 1))), 1.0, 0.0).astype(BF16)
    t_spare[...] = jnp.where(
        named_t & (at_t == MAIN + (col_i & (SPARE - 1))), 1.0, 0.0
    ).astype(BF16)

    big_i = lax.broadcasted_iota(jnp.int32, (GS, GM), 1)
    small_i = lax.broadcasted_iota(jnp.int32, (GS, GM), 0)
    big_t = lax.broadcasted_iota(jnp.int32, (GM, GS), 0)
    small_t = lax.broadcasted_iota(jnp.int32, (GM, GS), 1)

    def unfold(g):
        want = (small_i // SPARE) * MAIN + g * SPARE + (small_i & (SPARE - 1))
        return jnp.where(big_i == want, 1.0, 0.0).astype(BF16)

    def refold(g):
        want = (small_t // SPARE) * MAIN + g * SPARE + (small_t & (SPARE - 1))
        return jnp.where(big_t == want, 1.0, 0.0).astype(BF16)

    def wait_block(slot, way, out, into, send, recv):
        @pl.when(slot < own)
        def _():
            move(slot, way, out, into, send, recv).wait_recv()

    def unpack(into, chunk, dest, base):
        blocks = into.at[pl.ds(chunk * GROUP, GROUP)]
        dest[pl.ds(base, GM), :] = blocks[:, :, 0:width].reshape(GM, width)
        spare = blocks[:, :, width:].reshape(GM, fold)
        for g in range(FOLD):
            dest[pl.ds(base + GM, GS), pl.ds(g * fold, fold)] = dot(unfold(g), spare).astype(BF16)

    loads[2].wait()
    loads[3].wait()

    def forward(chunk, carry):
        for b in range(GROUP):
            wait_block(chunk * GROUP + b, 1, x_out, x_in, xs_sem, xr_sem)
        base = pl.multiple_of(chunk * GROWS, GROWS)
        unpack(x_in, chunk, xs, 0)
        both = dot(xs[...], wgu[...])
        pre[pl.ds(base, GROWS), :] = both
        gate = both[:, 0:ff]
        hidden[pl.ds(base, GROWS), :] = (gate * jax.nn.sigmoid(gate) * both[:, ff:]).astype(BF16)
        return carry

    lax.fori_loop(0, CHUNKS, forward, 0)

    @pl.when(ex == NEWS)
    def _():
        pl.semaphore_wait(barrier, 2 * (SIDE - 1))
        for e in range(PEERS):
            if e != NEWS:
                pl.semaphore_signal(dp_go, inc=1, device_id=(dp, e), device_id_type=MESH)

    loads[4].wait()

    def take(chunk, carry):
        for b in range(GROUP):
            wait_block(chunk * GROUP + b, 1, c_out, c_in, cs_sem, cr_sem)
        unpack(c_in, chunk, scaled, pl.multiple_of(chunk * GROWS, GROWS))
        return carry

    def backward(chunk, carry):
        base = pl.multiple_of(chunk * GROWS, GROWS)
        back = dot(scaled[pl.ds(base, GROWS), :], wd[...], NT)
        gate = pre[pl.ds(base, GROWS), 0:ff]
        up = pre[pl.ds(base, GROWS), ff:]
        sig = jax.nn.sigmoid(gate)
        gate_grad = (back * up * sig * (1.0 + gate * (1.0 - sig))).astype(BF16)
        up_grad = (back * (gate * sig)).astype(BF16)
        grads = jnp.concatenate([gate_grad, up_grad], axis=1)
        folded = jnp.zeros((GM, fold), F32)
        for g in range(FOLD):
            cols = pl.ds(g * fold, fold)
            pair = dot(grads, wgu[cols, :], NT).astype(BF16)
            r_out[pl.ds(chunk * GROUP, GROUP), :, cols] = pair[0:GM].reshape(GROUP, MAIN, fold)
            folded = folded + dot(refold(g), pair[GM:])
        r_out[pl.ds(chunk * GROUP, GROUP), :, pl.ds(width, fold)] = folded.astype(BF16).reshape(
            GROUP, MAIN, fold
        )
        return carry

    def send_back(chunk, carry):
        for b in range(GROUP):
            slot = chunk * GROUP + b

            @pl.when(slot < own)
            def _():
                move(slot, -1, r_out, r_in, rs_sem, rr_sem).start()

        return carry

    def both_steps(chunk, carry):
        return backward(chunk, take(chunk, carry))

    half = part // (2 * SIDE)

    def share(k, peer, at_axis, out, into, send, recv):
        return pltpu.make_async_remote_copy(
            src_ref=out.at[(at_axis + k) & (SIDE - 1)],
            dst_ref=into.at[k - 1],
            send_sem=send.at[k - 1],
            recv_sem=recv.at[k - 1],
            device_id=peer(k),
            device_id_type=MESH,
        )

    def outer(step, carry):
        k = (4 - (step + 1) // 2) * (2 * (step & 1) - 1) & (SIDE - 1)
        zz = (z + k) & (SIDE - 1)
        cols = pl.ds(pl.multiple_of(zz * part, part), part)
        term = dot(scaled[:, cols], hidden[...], TN).astype(BF16).reshape(SIDE, 2, half, ff)
        for xx in range(SIDE):
            dt_a[xx, zz] = term[xx, 0]
        dt_b[zz] = term[:, 1]

        @pl.when(step < SIDE - 1)
        def _():
            share(k, z_peer, z, dt_b, r_b, b1s, b1r).start()

        return carry

    order = (4, 3, 5, 2, 6, 1, 7)
    lax.fori_loop(0, CHUNKS // 2, both_steps, 0)
    lax.fori_loop(CHUNKS // 2, CHUNKS, take, 0)
    lax.fori_loop(0, CHUNKS // 2, send_back, 0)

    @pl.when(ex != NEWS)
    def _():
        pl.semaphore_wait(dp_go, 1)

    lax.fori_loop(0, SIDE, outer, 0)
    for k in order:
        share(k, x_peer, x, dt_a, r_a, a1s, a1r).start()
    lax.fori_loop(
        CHUNKS // 2, CHUNKS, lambda chunk, carry: send_back(chunk, backward(chunk, carry)), 0
    )
    r_in[own] = r_out[own]

    for k in order:
        share(k, x_peer, x, dt_a, r_a, a1s, a1r).wait_recv()
    total = dt_a[x].astype(F32)
    for k in range(SIDE - 1):
        total = total + r_a[k].astype(F32)
    s_a[...] = total.astype(BF16)
    for k in order:
        share(k, z_peer, z, s_a, q_a, a2s, a2r).start()
    for k in order:
        share(k, z_peer, z, dt_b, r_b, b1s, b1r).wait_recv()
    total = dt_b[z].astype(F32)
    for k in range(SIDE - 1):
        total = total + r_b[k].astype(F32)
    s_b[...] = total.astype(BF16)
    for k in order:
        share(k, x_peer, x, s_b, q_b, b2s, b2r).start()
    for slot in range(PEERS - 1):
        move(slot, 1, x_out, x_in, xs_sem, xr_sem).wait_send()
        move(slot, 1, c_out, c_in, cs_sem, cr_sem).wait_send()
    for slot in range(PEERS - 1):
        move(slot, -1, r_out, r_in, rs_sem, rr_sem).wait_recv()

    def leave(g):
        cols = pl.ds(g * fold, fold)
        return pltpu.make_async_copy(tg_out.at[:, cols], tg_ref.at[:, cols], leave_sem.at[g])

    col_piece = (lax.broadcasted_iota(jnp.int32, (rows, nrow), 1) & (MAIN - 1)) // SPARE
    spare = r_in[:, :, width:].reshape(nrow, fold)
    for g in range(FOLD):
        cols = slice(g * fold, (g + 1) * fold)
        main = r_in[:, :, cols].reshape(nrow, fold)
        pick_g = jnp.where(col_piece == g, t_spare[...].astype(F32), 0.0).astype(BF16)
        tg_out[:, cols] = (dot(t_main[...], main) + dot(pick_g, spare)).astype(BF16)
        leave(g).start()

    for k in order:
        share(k, z_peer, z, s_a, q_a, a2s, a2r).wait_recv()
        share(k, x_peer, x, s_b, q_b, b2s, b2r).wait_recv()
    total = s_a[z].astype(F32)
    for k in range(SIDE - 1):
        total = total + q_a[k].astype(F32)
    dg_ref[0:half, :] = total
    total = s_b[x].astype(F32)
    for k in range(SIDE - 1):
        total = total + q_b[k].astype(F32)
    dg_ref[half:, :] = total

    for k in order:
        share(k, x_peer, x, dt_a, r_a, a1s, a1r).wait_send()
        share(k, z_peer, z, dt_b, r_b, b1s, b1r).wait_send()
        share(k, z_peer, z, s_a, q_a, a2s, a2r).wait_send()
        share(k, x_peer, x, s_b, q_b, b2s, b2r).wait_send()
    for slot in range(PEERS - 1):
        move(slot, -1, r_out, r_in, rs_sem, rr_sem).wait_send()
    for g in range(FOLD):
        leave(g).wait()


def hand_over(tg_in, dg_in, tg_ref, dg_ref, tg_held, in_sem, out_sem):
    step = tg_held.shape[0] // FOLD
    coming, going = [], []
    for g in range(FOLD):
        some = pl.ds(g * step, step)
        coming.append(pltpu.make_async_copy(tg_in.at[some], tg_held.at[some], in_sem.at[g]))
        going.append(pltpu.make_async_copy(tg_held.at[some], tg_ref.at[some], out_sem.at[g]))
    for copy in coming:
        copy.start()
    going.append(pltpu.make_async_copy(dg_in, dg_ref, out_sem.at[FOLD]))
    going[FOLD].start()
    for g in range(FOLD):
        coming[g].wait()
        going[g].start()
    for copy in going:
        copy.wait()


def per_device(tokens, expert_index, gate_weights, cotangent, w_gate, w_up, w_down):
    rows, width = tokens.shape
    ff = w_gate.shape[2]
    wide = width + width // FOLD
    half = width // (2 * SIDE * SIDE)
    vmem = pl.BlockSpec(memory_space=pltpu.VMEM)
    hbm = pl.BlockSpec(memory_space=pl.ANY)
    blocks = pltpu.VMEM((PEERS, MAIN, wide), BF16)
    dma = pltpu.SemaphoreType.DMA
    token_grad, down_t = pl.pallas_call(
        body,
        out_shape=(
            jax.ShapeDtypeStruct((rows, width), BF16),
            jax.ShapeDtypeStruct((2 * half, ff), F32),
        ),
        in_specs=[vmem, vmem, hbm, hbm, hbm, hbm, hbm],
        out_specs=(hbm, vmem),
        scratch_shapes=[
            pltpu.VMEM((rows, width), BF16),
            pltpu.VMEM((rows, width), BF16),
            pltpu.VMEM((width, 2 * ff), BF16),
            pltpu.VMEM((ff, width), BF16),
            blocks, blocks, blocks, blocks, blocks, blocks,
            pltpu.VMEM((rows, PEERS * MAIN), BF16),
            pltpu.VMEM((rows, PEERS * MAIN), BF16),
            pltpu.VMEM((GROWS, width), BF16),
            pltpu.VMEM((CHUNKS * GROWS, 2 * ff), F32),
            pltpu.VMEM((CHUNKS * GROWS, width), BF16),
            pltpu.VMEM((CHUNKS * GROWS, ff), BF16),
            pltpu.VMEM((SIDE, SIDE, half, ff), BF16),
            pltpu.VMEM((SIDE, SIDE, half, ff), BF16),
            pltpu.VMEM((SIDE - 1, SIDE, half, ff), BF16),
            pltpu.VMEM((SIDE - 1, SIDE, half, ff), BF16),
            pltpu.VMEM((SIDE, half, ff), BF16),
            pltpu.VMEM((SIDE, half, ff), BF16),
            pltpu.VMEM((SIDE - 1, half, ff), BF16),
            pltpu.VMEM((SIDE - 1, half, ff), BF16),
            dma((5,)),
            dma((PEERS,)), dma((PEERS,)), dma((PEERS,)), dma((PEERS,)), dma((PEERS,)), dma((PEERS,)),
            dma((SIDE - 1,)), dma((SIDE - 1,)), dma((SIDE - 1,)), dma((SIDE - 1,)),
            dma((SIDE - 1,)), dma((SIDE - 1,)), dma((SIDE - 1,)), dma((SIDE - 1,)),
            pltpu.SemaphoreType.REGULAR, pltpu.SemaphoreType.REGULAR,
            pltpu.VMEM((rows, width), BF16), dma((FOLD,)),
        ],
        compiler_params=pltpu.CompilerParams(
            collective_id=0, has_side_effects=True, vmem_limit_bytes=56 << 20
        ),
        cost_estimate=pl.CostEstimate(
            flops=3 * 10**9, bytes_accessed=8 * 10**6, transcendentals=250000
        ),
    )(
        expert_index.T, gate_weights.T, tokens, cotangent, w_gate[0], w_up[0], w_down[0]
    )
    token_grad, down_t = pl.pallas_call(
        hand_over,
        out_shape=(
            jax.ShapeDtypeStruct((rows, width), BF16),
            jax.ShapeDtypeStruct((2 * half, ff), F32),
        ),
        in_specs=[hbm, vmem],
        out_specs=(hbm, hbm),
        scratch_shapes=[pltpu.VMEM((rows, width), BF16), dma((FOLD,)), dma((FOLD + 1,))],
    )(token_grad, down_t)
    return token_grad, down_t.T[None]


def solution(mesh):
    token_spec = P(("dp", "expert"), None)
    weight_spec = P("expert", None, None)
    return jax.shard_map(
        per_device,
        mesh=mesh,
        in_specs=(token_spec,) * 4 + (weight_spec,) * 3,
        out_specs=(token_spec, P("expert", None, "dp")),
        check_vma=False,
    )
```
